128 devices in a mesh: grp: 4 (over x), dev: 32 (over y, z, core).
Axes of the slice: x: 4, y: 4, z: 4, core: 2. Of those that a mesh axis runs over, the one named last changes fastest.
Arguments:
- parents: bfloat16 [1024, 2, 2, 96, 192], P(('grp', 'dev')), may hold values from -6 to 6
- theta_table: bfloat16 [192, 96], replicated, may hold values from -0.625 to 0.625
- azimuth_table: bfloat16 [192, 384], replicated, may hold values from -0.4375 to 0.4375
- phase_angle: float32 [8, 73728], replicated, may hold values from -3.140625 to 3.140625
- translators: float32 [316, 2, 73728], P(None, None, ('grp', 'dev')), may hold values from -0.24 to 0.24
- parent_slot: int32 [1024], P(('grp', 'dev')), may hold values from 0 to 2, as said below
- parent_octant: int32 [1024], P(('grp', 'dev')), may hold values from 0 to 7
- top_box: int32 [256], replicated, may hold values from 0 to 63, as said below
- far_source: int32 [64, 32], replicated, may hold values from 0 to 63, as said below
- far_kind: int32 [64, 32], replicated, may hold values from 0 to 315
Outputs:
- incoming: bfloat16 [1024, 2, 2, 96, 192], P(('grp', 'dev'))
The draws below stay inside these ranges and needn't reach their ends.
Inputs may be any that keep to these rules, and one draw needn't show every extreme that they name: `parent_slot`: 2 marks an empty parent slot; on each device the used slots come first. `top_box`: every top box is named by exactly 4 slots. `far_source`: the entries of a row are distinct and never the row's own box.
All inputs are finite; a program needn't handle non-finite values.
Results may differ from the reference program's by a relative error of at most 0.009.
Values may be sent and summed in bfloat16 or wider, within the bound.
A program may use at most 192 MiB of HBM per device.

```python
import jax
import jax.numpy as jnp
from jax import lax

COLUMNS = 2
PAR_DEV = 8
LOWER_THETA = 96
LOWER_PHI = 192
TOP_THETA = 192
TOP_PHI = 384
TOP_SLOTS = 2
KINDS = 316
SAMPLES = 73728
PARENTS = 1024
ALL_SLOTS = 256
TOP_BOXES = 64
FAR_COUNT = 32


def draw_parent_slot(key, part):
    key = jax.random.fold_in(key, 11)
    first_key, second_key = jax.random.split(key)
    device_count = PARENTS // PAR_DEV
    filled = jax.random.randint(first_key, (device_count, 1), 1, PAR_DEV + 1)
    picks = jax.random.randint(second_key, (device_count, PAR_DEV), 0, TOP_SLOTS)
    position = jnp.arange(PAR_DEV)[None, :]
    return jnp.where(position < filled, picks, TOP_SLOTS).reshape(-1).astype(jnp.int32)


def draw_top_box(key, part):
    key = jax.random.fold_in(key, 23)
    order = jax.random.permutation(key, ALL_SLOTS)
    return (order % TOP_BOXES).astype(jnp.int32)


def draw_far_source(key, part):
    key = jax.random.fold_in(key, 37)
    row_keys = jax.random.split(key, TOP_BOXES)
    picked = jax.vmap(lambda row_key: jax.random.permutation(row_key, TOP_BOXES - 1)[:FAR_COUNT])(row_keys)
    owner = jnp.arange(TOP_BOXES)[:, None]
    return (picked + (picked >= owner).astype(picked.dtype)).astype(jnp.int32)


def set_ends(values, rng, least, largest):
    longest = values.shape.index(max(values.shape))
    spots = []
    for shift in (0, 1):
        where = [jax.random.randint(jax.random.fold_in(rng, axis), (), 0, length) for axis, length in enumerate(values.shape)]
        where[longest] = (where[longest] + shift) % values.shape[longest]
        spots.append(tuple(where))
    return values.at[spots[0]].set(least).at[spots[1]].set(largest)


def level_of(rng, dims, cuts, low, high):
    gain, own = 1.0, jax.random.fold_in(rng, 6)
    for dim, parts in cuts:
        steps = jnp.exp(jax.random.uniform(jax.random.fold_in(own, dim), (parts,), jnp.float32, low / len(cuts), high / len(cuts)))
        gain = gain * jnp.repeat(steps, dims[dim] // parts).reshape([-1 if axis == dim else 1 for axis in range(len(dims))])
    return gain


def normal_values(rng, extent, deviation, bound, cuts=(), held_as=jnp.bfloat16):
    gain = level_of(rng, extent, cuts, -0.22, 0.18) if cuts else 1.0
    entries = jax.random.normal(rng, extent, jnp.float32) * deviation * gain
    return jnp.minimum(jnp.maximum(entries, -bound), bound).astype(held_as)


def setup_inputs(seed: int = 0) -> dict:
    key_of = jax.random.split(jax.random.key(seed), 11)
    parents = normal_values(key_of[0], (PARENTS, 2, COLUMNS, LOWER_THETA, LOWER_PHI), 1.0, 6.0, ((0, 128),))
    theta_table = normal_values(key_of[1], (TOP_THETA, LOWER_THETA), LOWER_THETA ** -0.5, 0.625)
    azimuth_table = normal_values(key_of[2], (LOWER_PHI, TOP_PHI), LOWER_PHI ** -0.5, 0.4375)
    phase_angle = jnp.clip(jax.random.uniform(key_of[3], (8, SAMPLES), jnp.float32, -3.140625, 3.140625), -3.140625, 3.140625)
    translators = normal_values(key_of[4], (KINDS, 2, SAMPLES), 0.04, 0.24, ((2, 128),), jnp.float32)
    parent_slot = draw_parent_slot(jax.random.fold_in(key_of[10], 71), 0)
    parent_octant = set_ends(jax.random.randint(key_of[6], (PARENTS,), 0, 8), jax.random.fold_in(key_of[6], 1), 0, 7).astype(jnp.int32)
    top_box = draw_top_box(jax.random.fold_in(key_of[10], 71), 0)
    far_source = draw_far_source(jax.random.fold_in(key_of[10], 71), 0)
    far_kind = set_ends(jax.random.randint(key_of[9], (TOP_BOXES, FAR_COUNT), 0, KINDS), jax.random.fold_in(key_of[9], 1), 0, KINDS - 1).astype(jnp.int32)
    return dict(parents=parents, theta_table=theta_table, azimuth_table=azimuth_table, phase_angle=phase_angle, translators=translators, parent_slot=parent_slot, parent_octant=parent_octant, top_box=top_box, far_source=far_source, far_kind=far_kind)


def rise_parent(parent, cosine, sine_table, theta_table, azimuth_table):
    widened = jnp.einsum('rctp,pq->rctq', parent.astype(jnp.float32), azimuth_table.astype(jnp.float32)).astype(jnp.bfloat16)
    lifted = jnp.einsum('st,rctq->rcsq', theta_table.astype(jnp.float32), widened.astype(jnp.float32))
    real_part = cosine * lifted[0] - sine_table * lifted[1]
    imag_part = sine_table * lifted[0] + cosine * lifted[1]
    return jnp.stack([real_part, imag_part])


def sink_parent(incident, cosine, sine_table, theta_table, azimuth_table):
    incident = incident.astype(jnp.float32)
    real_part = cosine * incident[0] + sine_table * incident[1]
    imag_part = cosine * incident[1] - sine_table * incident[0]
    turned = jnp.stack([real_part, imag_part]).astype(jnp.bfloat16)
    narrowed = jnp.einsum('st,rcsq->rctq', theta_table.astype(jnp.float32), turned.astype(jnp.float32)).astype(jnp.bfloat16)
    return jnp.einsum('rctq,pq->rctp', narrowed.astype(jnp.float32), azimuth_table.astype(jnp.float32))


def reference(parents, theta_table, azimuth_table, phase_angle, translators, parent_slot, parent_octant, top_box, far_source, far_kind):
    devices = PARENTS // PAR_DEV
    cosine_all = jnp.cos(phase_angle).reshape(8, TOP_THETA, TOP_PHI)
    sine_all = jnp.sin(phase_angle).reshape(8, TOP_THETA, TOP_PHI)
    grouped = parents.reshape(devices, PAR_DEV, 2, COLUMNS, LOWER_THETA, LOWER_PHI)
    slots_dev = parent_slot.reshape(devices, PAR_DEV)
    octants_dev = parent_octant.reshape(devices, PAR_DEV)

    def device_up(pieces):
        local, slots, octants = pieces
        totals = jnp.zeros((TOP_SLOTS, 2, COLUMNS, TOP_THETA, TOP_PHI), jnp.float32)
        for position in range(PAR_DEV):
            shifted = rise_parent(local[position], cosine_all[octants[position]], sine_all[octants[position]], theta_table, azimuth_table)
            chosen = (jnp.arange(TOP_SLOTS) == slots[position]).astype(jnp.float32)
            totals = totals + chosen[:, None, None, None, None] * shifted[None]
        return totals.astype(jnp.bfloat16).reshape(TOP_SLOTS, 2 * COLUMNS * SAMPLES)

    partial_value = lax.map(device_up, (grouped, slots_dev, octants_dev)).reshape(ALL_SLOTS, 2 * COLUMNS * SAMPLES)
    selector = (top_box[None, :] == jnp.arange(TOP_BOXES)[:, None]).astype(jnp.bfloat16)
    top_field = jnp.dot(selector, partial_value, preferred_element_type=jnp.float32).astype(jnp.bfloat16)
    top_field = top_field.reshape(TOP_BOXES, 2, COLUMNS, SAMPLES)

    def translate_one(pieces):
        sources, kinds = pieces
        pattern = top_field[sources].astype(jnp.float32)
        translator = translators[kinds]
        real_part = jnp.sum(translator[:, 0, None, :] * pattern[:, 0] - translator[:, 1, None, :] * pattern[:, 1], axis=0)
        imag_part = jnp.sum(translator[:, 0, None, :] * pattern[:, 1] + translator[:, 1, None, :] * pattern[:, 0], axis=0)
        return jnp.stack([real_part, imag_part]).astype(jnp.bfloat16)

    incoming_top = lax.map(translate_one, (far_source, far_kind))
    per_slot = incoming_top[top_box].reshape(devices, TOP_SLOTS, 2, COLUMNS, TOP_THETA, TOP_PHI)

    def device_down(pieces):
        slot_fields, slots, octants = pieces
        results = []
        for position in range(PAR_DEV):
            target = jnp.minimum(slots[position], TOP_SLOTS - 1)
            usable = (slots[position] < TOP_SLOTS).astype(jnp.float32)
            result = sink_parent(slot_fields[target], cosine_all[octants[position]], sine_all[octants[position]], theta_table, azimuth_table)
            results.append((result * usable).astype(jnp.bfloat16))
        return jnp.stack(results)

    outputs = lax.map(device_down, (per_slot, slots_dev, octants_dev))
    return outputs.reshape(PARENTS, 2, COLUMNS, LOWER_THETA, LOWER_PHI)
```

```python
import jax
import jax.numpy as jnp
from jax import lax
from jax.experimental import pallas as pl
from jax.experimental.pallas import tpu as pltpu
from jax.sharding import PartitionSpec as P

MESH = pl.DeviceIdType.MESH
F32 = jnp.float32
BF16 = jnp.bfloat16
TOP_SLOTS = 2
LANES = 128
SINE_TERMS = (
    0.9999999957103306,
    -0.16666657960973935,
    0.00833305040018596,
    -0.00019809029932038968,
    2.6051282412897536e-06,
)
COSINE_TERMS = (
    0.9999999531875788,
    -0.49999904965506836,
    0.04166357656486354,
    -0.0013853649037081687,
    2.315275975496213e-05,
)


def horner(terms, z):
    total = terms[-1] * z + terms[-2]
    for term in terms[-3::-1]:
        total = total * z + term
    return total


def phase_tables(phase_ref, cos_ref, sin_ref, top_theta):
    def fill(row, carry):
        for tile in range(3):
            place = pl.ds(pl.multiple_of(row * 384 + tile * LANES, LANES), LANES)
            half = phase_ref[:, place] * 0.5
            square = half * half
            sine = horner(SINE_TERMS, square) * half
            cosine = horner(COSINE_TERMS, square)
            rows = pl.ds(row, 8, stride=193)
            sin_ref[tile, rows, :] = 2.0 * sine * cosine
            cos_ref[tile, rows, :] = 1.0 - 2.0 * sine * sine
        return carry

    lax.fori_loop(0, top_theta, fill, 0, unroll=4)


def up_kernel(
    slot_ref, octant_ref, parents_ref, theta_ref, azimuth_ref, phase_ref,
    wire_ref, cos_ref, sin_ref, total_ref,
):
    top_theta, lower_theta = theta_ref.shape
    lower_phi = azimuth_ref.shape[0]
    phase_tables(phase_ref, cos_ref, sin_ref, top_theta)
    total_ref[...] = jnp.zeros_like(total_ref)

    def rise(n, carry):
        parent = parents_ref[n].reshape(4 * lower_theta, lower_phi)
        wide = jnp.dot(parent, azimuth_ref[...], preferred_element_type=F32).astype(BF16)
        slot = slot_ref[n]
        octant = octant_ref[n]
        turn_rows = pl.ds(octant * 193, top_theta)
        for tile in range(3):
            piece = wide[:, tile * LANES : (tile + 1) * LANES]
            piece = jnp.concatenate(
                [piece[k * lower_theta : (k + 1) * lower_theta] for k in range(4)], axis=1
            )
            lifted = jnp.dot(theta_ref[...], piece, preferred_element_type=F32)
            cosine = cos_ref[tile, turn_rows, :]
            sine = sin_ref[tile, turn_rows, :]
            for c in range(2):
                real = lifted[:, c * LANES : (c + 1) * LANES]
                imag = lifted[:, (2 + c) * LANES : (3 + c) * LANES]
                rows = pl.ds((slot * 4 + c) * 193, top_theta)
                total_ref[tile, rows, :] += cosine * real - sine * imag
                rows = pl.ds((slot * 4 + 2 + c) * 193, top_theta)
                total_ref[tile, rows, :] += sine * real + cosine * imag
        return carry

    lax.fori_loop(0, parents_ref.shape[0], rise, 0)

    def pack(pair, carry):
        tiles = [
            total_ref[tile, pl.ds(pair * 3 + row, 8, stride=193), :]
            for row in range(3)
            for tile in range(3)
        ]
        line = jnp.concatenate(tiles, axis=1).astype(BF16)
        wire_ref[pair * 2, :, 0:576] = line[:, 0:576]
        wire_ref[pair * 2 + 1, :, 0:576] = line[:, 576:1152]
        return carry

    lax.fori_loop(0, wire_ref.shape[0] // 2, pack, 0, unroll=2)


def translate_kernel(
    source_ref, kind_ref, box_column_ref, box_row_ref, received_ref, translators_ref,
    wire_ref, trans_ref, field_ref, done_ref, flat_ref,
):
    kinds = translators_ref.shape[0]
    devices = received_ref.shape[0]
    rows_in = devices * 8
    rows_box = flat_ref.shape[0]

    def arrange(group, carry):
        block = translators_ref[pl.ds(group * 4, 4)].reshape(8, 576)
        for k in range(8):
            trans_ref[pl.ds(group * 72 + k, 8, stride=9), 0:72] = block[:, 72 * k : 72 * k + 72]
        return carry

    lax.fori_loop(0, 76, arrange, 0, unroll=4)
    for g in (76, 77, 78):
        arrange(g, 0)
    up_row = lax.broadcasted_iota(jnp.int32, (rows_box, rows_in), 0)
    up_hot = jnp.where(box_row_ref[...] == up_row, 1.0, 0.0).astype(BF16)
    for tile in range(5):
        lanes = slice(tile * LANES, (tile + 1) * LANES)
        piece = received_ref[:, :, lanes].reshape(rows_in, LANES)
        top = jnp.dot(up_hot, piece, preferred_element_type=F32)
        flat_ref[:, lanes] = top.astype(BF16).astype(F32)

    def spread(group, carry):
        block = flat_ref[pl.ds(pl.multiple_of(group * 8, 8), 8), :]
        for k in range(8):
            field_ref[pl.ds(group * 72 + k, 8, stride=9), :] = block[:, 72 * k : 72 * k + LANES]
        return carry

    lax.fori_loop(0, rows_box // 8, spread, 0, unroll=4)

    def box(b, carry):
        def far(step, sums):
            sums = list(sums)
            for inner in range(8):
                spot = b * 32 + step * 8 + inner
                source = source_ref[spot] * 36
                kind = kind_ref[spot] * 18
                trans_real = trans_ref[pl.ds(kind, 8), :]
                trans_imag = trans_ref[pl.ds(kind + 9, 8), :]
                parts = [
                    field_ref[pl.ds(source + 9 * k, 8), :] for k in range(4)
                ]
                for c in range(2):
                    sums[c] += trans_real * parts[c] - trans_imag * parts[2 + c]
                    sums[2 + c] += trans_real * parts[2 + c] + trans_imag * parts[c]
            return tuple(sums)

        sums = lax.fori_loop(0, 4, far, (jnp.zeros((8, LANES), F32),) * 4)
        for k in range(4):
            done_ref[pl.ds(b * 36 + 9 * k, 8), :] = sums[k]
        return carry

    lax.fori_loop(0, rows_box // 4, box, 0)

    def gather(group, carry):
        pieces = [done_ref[pl.ds(group * 72 + k, 8, stride=9), :][:, 0:72] for k in range(8)]
        pieces.append(jnp.zeros((8, 64), F32))
        flat_ref[pl.ds(pl.multiple_of(group * 8, 8), 8), :] = jnp.concatenate(pieces, axis=1)
        return carry

    lax.fori_loop(0, rows_box // 8, gather, 0, unroll=4)
    down_column = lax.broadcasted_iota(jnp.int32, (rows_in, rows_box), 1)
    down_hot = jnp.where(box_column_ref[...] == down_column, 1.0, 0.0).astype(BF16)
    for tile in range(5):
        lanes = slice(tile * LANES, (tile + 1) * LANES)
        piece = flat_ref[:, lanes].astype(BF16)
        out = jnp.dot(down_hot, piece, preferred_element_type=F32).astype(BF16)
        wire_ref[:, :, lanes] = out.reshape(devices, 8, LANES)


def down_kernel(
    slot_ref, octant_ref, received_ref, theta_ref, azimuth_ref, phase_ref,
    out_ref, cos_ref, sin_ref, field_ref, narrow_ref,
):
    lower_theta, top_theta = theta_ref.shape
    lower_phi = azimuth_ref.shape[1]
    phase_tables(phase_ref, cos_ref, sin_ref, top_theta)

    def unpack(pair, carry):
        line = jnp.concatenate(
            [received_ref[pair * 2].astype(F32)[:, 0:576], received_ref[pair * 2 + 1].astype(F32)[:, 0:576]],
            axis=1,
        )
        for row in range(3):
            for tile in range(3):
                at = (row * 3 + tile) * LANES
                field_ref[tile, pl.ds(pair * 3 + row, 8, stride=193), :] = line[:, at : at + LANES]
        return carry

    lax.fori_loop(0, received_ref.shape[0] // 2, unpack, 0, unroll=4)

    def sink(n, carry):
        slot = slot_ref[n]
        target = jnp.minimum(slot, TOP_SLOTS - 1)
        usable = jnp.where(slot < TOP_SLOTS, 1.0, 0.0).astype(F32)
        turn_rows = pl.ds(octant_ref[n] * 193, top_theta)
        for tile in range(3):
            cosine = cos_ref[tile, turn_rows, :]
            sine = sin_ref[tile, turn_rows, :]
            real_parts, imag_parts = [], []
            for c in range(2):
                rows = pl.ds((target * 4 + c) * 193, top_theta)
                real = field_ref[tile, rows, :]
                rows = pl.ds((target * 4 + 2 + c) * 193, top_theta)
                imag = field_ref[tile, rows, :]
                real_parts.append((cosine * real + sine * imag).astype(BF16))
                imag_parts.append((cosine * imag - sine * real).astype(BF16))
            turned = jnp.concatenate(real_parts + imag_parts, axis=1)
            narrowed = jnp.dot(theta_ref[...], turned, preferred_element_type=F32).astype(BF16)
            for k in range(4):
                narrow_ref[
                    k * lower_theta : (k + 1) * lower_theta, tile * LANES : (tile + 1) * LANES
                ] = narrowed[:, k * LANES : (k + 1) * LANES]
        result = jnp.dot(narrow_ref[...], azimuth_ref[...], preferred_element_type=F32)
        out_ref[n] = (result * usable).astype(BF16).reshape(2, 2, lower_theta, lower_phi)
        return carry

    lax.fori_loop(0, out_ref.shape[0], sink, 0)


def exchange_kernel(send_ref, receive_ref, own_sem, send_sem, receive_sem):
    count = send_ref.shape[0]
    x = lax.axis_index("grp")
    rest = lax.axis_index("dev")
    y, z, core = rest // 8, lax.rem(rest, 8) // 2, lax.rem(rest, 2)
    me = x * 32 + rest

    def partner(k):
        step = lax.rem(k * 37, count)
        far = lax.rem(step, 32)
        to_x = lax.rem(x + step // 32, 4)
        to_y = lax.rem(y + far // 8, 4)
        to_z = lax.rem(z + lax.rem(far, 8) // 2, 4)
        to_rest = to_y * 8 + to_z * 2 + lax.rem(core + lax.rem(far, 2), 2)
        return (to_x, to_rest), to_x * 32 + to_rest

    barrier = pltpu.get_barrier_semaphore()

    def greet(k, carry):
        pl.semaphore_signal(barrier, inc=1, device_id=partner(k)[0], device_id_type=MESH)
        return carry

    lax.fori_loop(1, count, greet, 0)
    own = pltpu.make_async_copy(send_ref.at[me], receive_ref.at[me], own_sem)
    own.start()
    pl.semaphore_wait(barrier, count - 1)

    def send(k, carry):
        device, other = partner(k)
        pltpu.make_async_remote_copy(
            src_ref=send_ref.at[other],
            dst_ref=receive_ref.at[me],
            send_sem=send_sem,
            recv_sem=receive_sem,
            device_id=device,
            device_id_type=MESH,
        ).start()
        return carry

    lax.fori_loop(1, count, send, 0)
    own.wait()
    some = send_ref.at[pl.ds(1, count - 1)]
    pltpu.make_async_copy(some, some, send_sem).wait()
    some = receive_ref.at[pl.ds(1, count - 1)]
    pltpu.make_async_copy(some, some, receive_sem).wait()


VMEM = pl.BlockSpec(memory_space=pltpu.VMEM)
ANY = pl.BlockSpec(memory_space=pl.ANY)
SMEM = pl.BlockSpec(memory_space=pltpu.SMEM)
LIMIT = 56 * 1024 * 1024


def exchange(wire, which):
    return pl.pallas_call(
        exchange_kernel,
        out_shape=jax.ShapeDtypeStruct(wire.shape, wire.dtype),
        in_specs=[ANY],
        out_specs=ANY,
        scratch_shapes=[pltpu.SemaphoreType.DMA] * 3,
        compiler_params=pltpu.CompilerParams(
            collective_id=which, has_side_effects=True, vmem_limit_bytes=LIMIT
        ),
    )(wire)


def shards(
    parents,
    theta_table,
    azimuth_table,
    phase_angle,
    translators,
    parent_slot,
    parent_octant,
    top_box,
    far_source,
    far_kind,
):
    top_theta = theta_table.shape[0]
    devices = top_box.shape[0] // TOP_SLOTS
    boxes = far_source.shape[0]
    samples = translators.shape[2]
    params = pltpu.CompilerParams(vmem_limit_bytes=LIMIT)
    tables = [pltpu.VMEM((3, 8 * 193 + 8, LANES), F32)] * 2
    blocks = jax.ShapeDtypeStruct((devices, 8, 640), BF16)
    wire = pl.pallas_call(
        up_kernel,
        out_shape=blocks,
        in_specs=[SMEM, SMEM, VMEM, VMEM, VMEM, VMEM],
        out_specs=VMEM,
        scratch_shapes=tables + [pltpu.VMEM((3, 12 * 193 + 8, LANES), F32)],
        compiler_params=params,
    )(parent_slot, parent_octant, parents, theta_table, azimuth_table, phase_angle)
    received = exchange(wire, 0)
    places = (top_box[:, None] * 4 + jnp.arange(4)).reshape(-1)
    wire = pl.pallas_call(
        translate_kernel,
        out_shape=blocks,
        in_specs=[SMEM, SMEM, VMEM, VMEM, VMEM, VMEM],
        out_specs=VMEM,
        scratch_shapes=[
            pltpu.VMEM((translators.shape[0] * 18 + 8, LANES), F32),
            pltpu.VMEM((boxes * 36 + 8, LANES), F32),
            pltpu.VMEM((boxes * 36 + 8, LANES), F32),
            pltpu.VMEM((boxes * 4, 640), F32),
        ],
        compiler_params=params,
    )(
        far_source.reshape(-1),
        far_kind.reshape(-1),
        places[:, None],
        places[None, :],
        received,
        translators,
    )
    received = exchange(wire, 1)
    return pl.pallas_call(
        down_kernel,
        out_shape=jax.ShapeDtypeStruct(parents.shape, BF16),
        in_specs=[SMEM, SMEM, VMEM, VMEM, VMEM, VMEM],
        out_specs=VMEM,
        scratch_shapes=tables
        + [
            pltpu.VMEM((3, 8 * 193 + 8, LANES), F32),
            pltpu.VMEM((4 * theta_table.shape[1], azimuth_table.shape[1]), BF16),
        ],
        compiler_params=params,
    )(parent_slot, parent_octant, received, theta_table.T, azimuth_table.T, phase_angle)


def solution(mesh):
    placed = (
        P(("grp", "dev"), None, None, None, None),
        P(),
        P(),
        P(),
        P(None, None, ("grp", "dev")),
        P(("grp", "dev")),
        P(("grp", "dev")),
        P(),
        P(),
        P(),
    )
    return jax.shard_map(
        shards,
        mesh=mesh,
        in_specs=placed,
        out_specs=P(("grp", "dev"), None, None, None, None),
        check_vma=False,
    )
```

```python
import jax
import jax.numpy as jnp
from jax import lax
from jax.experimental import pallas as pl
from jax.experimental.pallas import tpu as pltpu
from jax.sharding import PartitionSpec as P

MESH = pl.DeviceIdType.MESH
F32 = jnp.float32
BF16 = jnp.bfloat16
TOP_SLOTS = 2
LANES = 128
SINE_TERMS = (
    0.9999999957103306,
    -0.16666657960973935,
    0.00833305040018596,
    -0.00019809029932038968,
    2.6051282412897536e-06,
)
COSINE_TERMS = (
    0.9999999531875788,
    -0.49999904965506836,
    0.04166357656486354,
    -0.0013853649037081687,
    2.315275975496213e-05,
)


def horner(terms, z):
    total = terms[-1] * z + terms[-2]
    for term in terms[-3::-1]:
        total = total * z + term
    return total


BLOCK = 576
ODD = 193
COLUMNS = 2


def kernel(
    slot_ref, octant_ref, source_ref, kind_ref, place_ref, theta_ref, azimuth_ref,
    phase_hbm, parents_hbm, translators_hbm,
    out_ref,
    phase_ref, parents_ref, translators_ref, cos_ref, sin_ref, total_ref,
    up_send, up_got, down_send, down_got,
    trans_ref, field_ref, done_ref, flat_ref, up_hot, down_hot, theta_flip, narrow_ref,
    in_sem, own_sem, send_sem, got_sem,
):
    top_theta, lower_theta = theta_ref.shape
    lower_phi = azimuth_ref.shape[0]
    count = up_send.shape[1]
    pairs = count // 2
    parent_count = out_ref.shape[0]
    boxes = source_ref.shape[0]
    far_count = source_ref.shape[1]
    kinds = translators_ref.shape[0]

    x = lax.axis_index("grp")
    rest = lax.axis_index("dev")
    y, z, core = rest // 8, lax.rem(rest, 8) // 2, lax.rem(rest, 2)
    me = x * 32 + rest

    def chip(k):
        step = lax.rem(k * 37, pairs)
        to_x = lax.rem(x + step // 16, 4)
        to_y = lax.rem(y + lax.rem(step, 16) // 4, 4)
        to_z = lax.rem(z + lax.rem(step, 4), 4)
        return to_x, to_y * 8 + to_z * 2

    loads = [
        pltpu.make_async_copy(phase_hbm, phase_ref, in_sem.at[0]),
        pltpu.make_async_copy(parents_hbm, parents_ref, in_sem.at[1]),
        pltpu.make_async_copy(translators_hbm, translators_ref, in_sem.at[2]),
    ]
    for load in loads:
        load.start()

    barrier = pltpu.get_barrier_semaphore()

    def greet(k):
        to_x, to_rest = chip(k)
        for to_core in range(2):
            pl.semaphore_signal(
                barrier, inc=1, device_id=(to_x, to_rest + to_core), device_id_type=MESH
            )

    pl.semaphore_signal(barrier, inc=1, device_id=(x, rest + 1 - 2 * core), device_id_type=MESH)
    loads[0].wait()

    def fill(row):
        for tile in range(3):
            place = pl.ds(pl.multiple_of(row * 384 + tile * LANES, LANES), LANES)
            half = phase_ref[:, place] * 0.5
            square = half * half
            sine = horner(SINE_TERMS, square) * half
            cosine = horner(COSINE_TERMS, square)
            rows = pl.ds(row, 8, stride=ODD)
            sin_ref[tile, rows, :] = 2.0 * sine * cosine
            cos_ref[tile, rows, :] = 1.0 - 2.0 * sine * sine

    for row in range(3):
        fill(row)

    def fill_greet(k, carry):
        for inner in range(3):
            fill(k * 3 + inner)
        greet(k)
        return carry

    lax.fori_loop(1, pairs, fill_greet, 0)
    loads[1].wait()

    def send(out, got, block, device, side):
        pltpu.make_async_remote_copy(
            src_ref=out.at[block],
            dst_ref=got.at[me],
            send_sem=send_sem.at[side],
            recv_sem=got_sem.at[side],
            device_id=device,
            device_id_type=MESH,
        ).start()

    def send_pair(out, got, k, side):
        to_x, to_rest = chip(k)
        for to_core in range(2):
            device = (to_x, to_rest + to_core)
            send(out, got, to_x * 32 + to_rest + to_core, device, side)

    def send_own(out, got, side):
        send(out, got, me + 1 - 2 * core, (x, rest + 1 - 2 * core), side)
        pltpu.make_async_copy(out.at[me], got.at[me], own_sem.at[side]).start()

    def await_got(out, got, side):
        pltpu.make_async_copy(out.at[me], got.at[me], own_sem.at[side]).wait()
        some = got.at[pl.ds(1, count - 1)]
        pltpu.make_async_copy(some, some, got_sem.at[side]).wait()

    def rise(c):
        total_ref[...] = jnp.zeros_like(total_ref)

        def two(step, carry):
            wides, weights, turns = [], [], []
            for inner in range(2):
                n = step * 2 + inner
                slot = slot_ref[n]
                used = jnp.where(slot < TOP_SLOTS, 1.0, 0.0).astype(F32)
                parent = parents_ref[n, :, c].reshape(2 * lower_theta, lower_phi)
                wide = jnp.dot(parent, azimuth_ref[...], preferred_element_type=F32)
                wides.append((wide * used).astype(BF16))
                weights.append(jnp.where(slot == 1, 1.0, 0.0).astype(F32))
                turns.append(pl.ds(octant_ref[n] * ODD, top_theta))
            for tile in range(3):
                reals, imags = [], []
                for inner in range(2):
                    piece = wides[inner][:, tile * LANES : (tile + 1) * LANES]
                    piece = jnp.concatenate([piece[:lower_theta], piece[lower_theta:]], axis=1)
                    lifted = jnp.dot(theta_ref[...], piece, preferred_element_type=F32)
                    real, imag = lifted[:, :LANES], lifted[:, LANES:]
                    cosine = cos_ref[tile, turns[inner], :]
                    sine = sin_ref[tile, turns[inner], :]
                    reals.append(cosine * real - sine * imag)
                    imags.append(sine * real + cosine * imag)
                for part, (one, other) in enumerate((reals, imags)):
                    total_ref[tile, pl.ds(part * ODD, top_theta), :] += one + other
                    total_ref[tile, pl.ds((2 + part) * ODD, top_theta), :] += (
                        weights[0] * one + weights[1] * other
                    )
            return carry

        lax.fori_loop(0, parent_count // 2, two, 0)
        for tile in range(3):
            both = pl.ds(0, 2 * ODD)
            total_ref[tile, both, :] -= total_ref[tile, pl.ds(2 * ODD, 2 * ODD), :]

    def pack(c, to_x, to_rest):
        pair = to_x * 16 + to_rest // 2
        tiles = [
            total_ref[tile, pl.ds(pair * 3 + row, 4, stride=ODD), :]
            for row in range(3)
            for tile in range(3)
        ]
        line = jnp.concatenate(tiles, axis=1).astype(BF16)
        up_send[c, pair * 2, :, 0:BLOCK] = line[:, 0:BLOCK]
        up_send[c, pair * 2 + 1, :, 0:BLOCK] = line[:, BLOCK : 2 * BLOCK]

    rise(0)
    pl.semaphore_wait(barrier, count - 1)
    for c in range(COLUMNS):
        if c:
            rise(c)
        pack(c, x, y * 8 + z * 2)
        send_own(up_send.at[c], up_got.at[c], c)

        def pack_send(k, carry, c=c):
            pack(c, *chip(k))
            send_pair(up_send.at[c], up_got.at[c], k, c)
            return carry

        lax.fori_loop(1, pairs, pack_send, 0)

    loads[2].wait()

    def arrange(group):
        block = translators_ref[pl.ds(group * 4, 4)].reshape(8, BLOCK)
        for k in range(8):
            trans_ref[pl.ds(group * 72 + k, 8, stride=9), 0:72] = block[:, 72 * k : 72 * k + 72]

    def arrange_four(step, carry):
        for inner in range(4):
            arrange(step * 4 + inner)
        return carry

    lax.fori_loop(0, kinds // 16, arrange_four, 0)
    for group in range(kinds // 16 * 4, kinds // 4):
        arrange(group)
    hot = jnp.where(
        place_ref[...] == lax.broadcasted_iota(jnp.int32, up_hot.shape, 0), 1.0, 0.0
    ).astype(F32)
    up_hot[...] = hot.astype(BF16)
    down_hot[...] = hot.T.astype(BF16)
    theta_flip[...] = theta_ref[...].astype(F32).T.astype(BF16)

    for c in range(COLUMNS):
        await_got(up_send.at[c], up_got.at[c], c)
        for tile in range(5):
            lanes = slice(tile * LANES, (tile + 1) * LANES)
            piece = up_got[c, :, :, lanes].reshape(count * 4, LANES)
            top = jnp.dot(up_hot[...], piece, preferred_element_type=F32)
            flat_ref[:, lanes] = top.astype(BF16).astype(F32)

        def spread(step, carry):
            for inner in range(4):
                group = step * 4 + inner
                block = flat_ref[pl.ds(pl.multiple_of(group * 8, 8), 8), :]
                for k in range(8):
                    field_ref[pl.ds(group * 72 + k, 8, stride=9), :] = block[
                        :, 72 * k : 72 * k + LANES
                    ]
            return carry

        lax.fori_loop(0, boxes // 16, spread, 0)

        def box(b):
            def far(step, sums):
                sums = list(sums)
                for inner in range(16):
                    spot = step * 16 + inner
                    source = source_ref[b, spot] * 18
                    kind = kind_ref[b, spot] * 18
                    trans_real = trans_ref[pl.ds(kind, 8), :]
                    trans_imag = trans_ref[pl.ds(kind + 9, 8), :]
                    real = field_ref[pl.ds(source, 8), :]
                    imag = field_ref[pl.ds(source + 9, 8), :]
                    sums[0] += trans_real * real
                    sums[1] += trans_imag * imag
                    sums[2] += trans_real * imag
                    sums[3] += trans_imag * real
                return tuple(sums)

            sums = lax.fori_loop(0, far_count // 16, far, (jnp.zeros((8, LANES), F32),) * 4)
            done_ref[pl.ds(b * 18, 8), :] = sums[0] - sums[1]
            done_ref[pl.ds(b * 18 + 9, 8), :] = sums[2] + sums[3]

        if c == 0:

            def plain(b, carry):
                box(b)
                return carry

            lax.fori_loop(0, boxes, plain, 0)
        else:
            box(0)
            send_own(down_send.at[0], down_got.at[0], 2)

            def box_send(b, carry):
                box(b)
                send_pair(down_send.at[0], down_got.at[0], b, 2)
                return carry

            lax.fori_loop(1, boxes, box_send, 0)

        def gather(step, carry):
            for inner in range(4):
                group = step * 4 + inner
                pieces = [
                    done_ref[pl.ds(group * 72 + k, 8, stride=9), :][:, 0:72] for k in range(8)
                ]
                pieces.append(jnp.zeros((8, 64), F32))
                rows = pl.ds(pl.multiple_of(group * 8, 8), 8)
                flat_ref[rows, :] = jnp.concatenate(pieces, axis=1)
            return carry

        lax.fori_loop(0, boxes // 16, gather, 0)
        for tile in range(5):
            lanes = slice(tile * LANES, (tile + 1) * LANES)
            piece = flat_ref[:, lanes].astype(BF16)
            out = jnp.dot(down_hot[...], piece, preferred_element_type=F32).astype(BF16)
            down_send[c, :, :, lanes] = out.reshape(count, 4, LANES)

    send_own(down_send.at[1], down_got.at[1], 3)

    def last_send(k, carry):
        send_pair(down_send.at[1], down_got.at[1], k, 3)
        return carry

    lax.fori_loop(1, pairs, last_send, 0)

    for c in range(COLUMNS):
        await_got(down_send.at[c], down_got.at[c], 2 + c)

        def unpack(step, carry, c=c):
            for inner in range(2):
                pair = step * 2 + inner
                line = jnp.concatenate(
                    [
                        down_got[c, pair * 2].astype(F32)[:, 0:BLOCK],
                        down_got[c, pair * 2 + 1].astype(F32)[:, 0:BLOCK],
                    ],
                    axis=1,
                )
                for row in range(3):
                    for tile in range(3):
                        at = (row * 3 + tile) * LANES
                        total_ref[tile, pl.ds(pair * 3 + row, 4, stride=ODD), :] = line[
                            :, at : at + LANES
                        ]
            return carry

        lax.fori_loop(0, pairs // 2, unpack, 0)

        def sink(n, carry, c=c):
            slot = slot_ref[n]
            target = jnp.minimum(slot, TOP_SLOTS - 1) * 2
            usable = jnp.where(slot < TOP_SLOTS, 1.0, 0.0).astype(F32)
            turn = pl.ds(octant_ref[n] * ODD, top_theta)
            for tile in range(3):
                cosine = cos_ref[tile, turn, :]
                sine = sin_ref[tile, turn, :]
                real = total_ref[tile, pl.ds(target * ODD, top_theta), :]
                imag = total_ref[tile, pl.ds((target + 1) * ODD, top_theta), :]
                turned = jnp.concatenate(
                    [
                        (cosine * real + sine * imag).astype(BF16),
                        (cosine * imag - sine * real).astype(BF16),
                    ],
                    axis=1,
                )
                narrowed = jnp.dot(theta_flip[...], turned, preferred_element_type=F32)
                narrowed = narrowed.astype(BF16)
                lanes = slice(tile * LANES, (tile + 1) * LANES)
                narrow_ref[:lower_theta, lanes] = narrowed[:, :LANES]
                narrow_ref[lower_theta:, lanes] = narrowed[:, LANES:]
            result = lax.dot_general(
                narrow_ref[...],
                azimuth_ref[...],
                (((1,), (1,)), ((), ())),
                preferred_element_type=F32,
            )
            out_ref[n, :, c] = (result * usable).astype(BF16).reshape(2, lower_theta, lower_phi)
            return carry

        lax.fori_loop(0, parent_count, sink, 0)

    for side, out in enumerate((up_send.at[0], up_send.at[1], down_send.at[0], down_send.at[1])):
        some = out.at[pl.ds(1, count - 1)]
        pltpu.make_async_copy(some, some, send_sem.at[side]).wait()


VMEM = pl.BlockSpec(memory_space=pltpu.VMEM)
SMEM = pl.BlockSpec(memory_space=pltpu.SMEM)
ANY = pl.BlockSpec(memory_space=pl.ANY)
LIMIT = 56 * 1024 * 1024


def shards(
    parents,
    theta_table,
    azimuth_table,
    phase_angle,
    translators,
    parent_slot,
    parent_octant,
    top_box,
    far_source,
    far_kind,
):
    top_theta, lower_theta = theta_table.shape
    devices = top_box.shape[0] // TOP_SLOTS
    boxes = far_source.shape[0]
    kinds = translators.shape[0]
    place = (top_box[:, None] * 2 + jnp.arange(2)).reshape(1, -1)
    wire = pltpu.VMEM((COLUMNS, devices, 4, 640), BF16)
    rows = pltpu.VMEM((boxes * 18 + 8, LANES), F32)
    return pl.pallas_call(
        kernel,
        out_shape=jax.ShapeDtypeStruct(parents.shape, BF16),
        in_specs=[SMEM] * 4 + [VMEM] * 3 + [ANY] * 3,
        out_specs=VMEM,
        scratch_shapes=[
            pltpu.VMEM(phase_angle.shape, F32),
            pltpu.VMEM(parents.shape, BF16),
            pltpu.VMEM(translators.shape, F32),
            pltpu.VMEM((3, 8 * ODD + 8, LANES), F32),
            pltpu.VMEM((3, 8 * ODD + 8, LANES), F32),
            pltpu.VMEM((3, 4 * ODD + 4, LANES), F32),
            wire,
            wire,
            wire,
            wire,
            pltpu.VMEM((kinds * 18 + 8, LANES), F32),
            rows,
            rows,
            pltpu.VMEM((boxes * 2, 640), F32),
            pltpu.VMEM((boxes * 2, devices * 4), BF16),
            pltpu.VMEM((devices * 4, boxes * 2), BF16),
            pltpu.VMEM((lower_theta, top_theta), BF16),
            pltpu.VMEM((2 * lower_theta, azimuth_table.shape[1]), BF16),
            pltpu.SemaphoreType.DMA((3,)),
            pltpu.SemaphoreType.DMA((4,)),
            pltpu.SemaphoreType.DMA((4,)),
            pltpu.SemaphoreType.DMA((4,)),
        ],
        compiler_params=pltpu.CompilerParams(
            collective_id=0, has_side_effects=True, vmem_limit_bytes=LIMIT
        ),
    )(
        parent_slot,
        parent_octant,
        far_source,
        far_kind,
        place,
        theta_table,
        azimuth_table,
        phase_angle,
        parents,
        translators,
    )


def solution(mesh):
    placed = (
        P(("grp", "dev"), None, None, None, None),
        P(),
        P(),
        P(),
        P(None, None, ("grp", "dev")),
        P(("grp", "dev")),
        P(("grp", "dev")),
        P(),
        P(),
        P(),
    )
    return jax.shard_map(
        shards,
        mesh=mesh,
        in_specs=placed,
        out_specs=P(("grp", "dev"), None, None, None, None),
        check_vma=False,
    )
```

```python
import jax
import jax.numpy as jnp
from jax import lax
from jax.experimental import pallas as pl
from jax.experimental.pallas import tpu as pltpu
from jax.sharding import PartitionSpec as P

MESH = pl.DeviceIdType.MESH
F32 = jnp.float32
BF16 = jnp.bfloat16
TOP_SLOTS = 2
LANES = 128
SINE_TERMS = (
    0.9999999957103306,
    -0.16666657960973935,
    0.00833305040018596,
    -0.00019809029932038968,
    2.6051282412897536e-06,
)
COSINE_TERMS = (
    0.9999999531875788,
    -0.49999904965506836,
    0.04166357656486354,
    -0.0013853649037081687,
    2.315275975496213e-05,
)


def horner(terms, z):
    total = terms[-1] * z + terms[-2]
    for term in terms[-3::-1]:
        total = total * z + term
    return total


BLOCK = 576
ODD = 193
COLUMNS = 2


def kernel(
    slot_ref, octant_ref, source_in, kind_in, place_ref, theta_ref, azimuth_ref,
    phase_hbm, parents_hbm, translators_hbm,
    out_ref,
    phase_ref, parents_ref, translators_ref, cos_ref, sin_ref, total_ref,
    up_send, up_got, down_send, down_got,
    scaled_ref, source_ref, kind_ref, trans_ref, field_ref, done_ref, flat_ref, up_hot, down_hot, theta_flip, narrow_ref,
    in_sem, own_sem, send_sem, got_sem,
):
    top_theta, lower_theta = theta_ref.shape
    lower_phi = azimuth_ref.shape[0]
    count = up_send.shape[1]
    pairs = count // 2
    parent_count = out_ref.shape[0]
    far_count, boxes = source_in.shape
    kinds = translators_ref.shape[0]

    x = lax.axis_index("grp")
    rest = lax.axis_index("dev")
    y, z, core = rest // 8, lax.rem(rest, 8) // 2, lax.rem(rest, 2)
    me = x * 32 + rest

    turn_x = [lax.rem(x + near, 4) for near in range(4)]

    def chip(far, near):
        to_y = lax.rem(y + near + far // 4, 4)
        to_z = lax.rem(z + near + lax.rem(far, 4), 4)
        return turn_x[near], to_y * 8 + to_z * 2

    loads = [
        pltpu.make_async_copy(phase_hbm, phase_ref, in_sem.at[0]),
        pltpu.make_async_copy(parents_hbm, parents_ref, in_sem.at[1]),
        pltpu.make_async_copy(translators_hbm, translators_ref, in_sem.at[2]),
    ]
    for load in loads:
        load.start()

    scaled_ref[0] = source_in[...] * 18
    scaled_ref[1] = kind_in[...] * 18
    loads.append(pltpu.make_async_copy(scaled_ref.at[0], source_ref, in_sem.at[3]))
    loads.append(pltpu.make_async_copy(scaled_ref.at[1], kind_ref, in_sem.at[4]))
    for load in loads[3:]:
        load.start()

    barrier = pltpu.get_barrier_semaphore()

    def greet(far, near):
        to_x, to_rest = chip(far, near)
        for to_core in range(2):
            pl.semaphore_signal(
                barrier, inc=1, device_id=(to_x, to_rest + to_core), device_id_type=MESH
            )

    pl.semaphore_signal(barrier, inc=1, device_id=(x, rest + 1 - 2 * core), device_id_type=MESH)
    loads[0].wait()

    def fill(row):
        for tile in range(3):
            place = pl.ds(pl.multiple_of(row * 384 + tile * LANES, LANES), LANES)
            half = phase_ref[:, place] * 0.5
            square = half * half
            sine = horner(SINE_TERMS, square) * half
            cosine = horner(COSINE_TERMS, square)
            rows = pl.ds(row, 8, stride=ODD)
            sin_ref[tile, rows, :] = 2.0 * sine * cosine
            cos_ref[tile, rows, :] = 1.0 - 2.0 * sine * sine

    def fill_greet(far, carry, first=0):
        for inner in range(12):
            fill(far * 12 + inner)
        for near in range(first, 4):
            greet(far, near)
        return carry

    fill_greet(0, 0, 1)
    lax.fori_loop(1, pairs // 4, fill_greet, 0)
    loads[1].wait()

    def send(out, got, block, device, side):
        pltpu.make_async_remote_copy(
            src_ref=out.at[block],
            dst_ref=got.at[me],
            send_sem=send_sem.at[side],
            recv_sem=got_sem.at[side],
            device_id=device,
            device_id_type=MESH,
        ).start()

    def send_pair(out, got, far, near, side):
        to_x, to_rest = chip(far, near)
        for to_core in range(2):
            device = (to_x, to_rest + to_core)
            send(out, got, to_x * 32 + to_rest + to_core, device, side)

    def send_own(out, got, side):
        send(out, got, me + 1 - 2 * core, (x, rest + 1 - 2 * core), side)
        pltpu.make_async_copy(out.at[me], got.at[me], own_sem.at[side]).start()

    def await_got(out, got, side):
        pltpu.make_async_copy(out.at[me], got.at[me], own_sem.at[side]).wait()
        some = got.at[pl.ds(1, count - 1)]
        pltpu.make_async_copy(some, some, got_sem.at[side]).wait()

    def rise(c):
        total_ref[...] = jnp.zeros_like(total_ref)

        def two(step, carry):
            wides, weights, turns = [], [], []
            for inner in range(2):
                n = step * 2 + inner
                slot = slot_ref[n]
                used = jnp.where(slot < TOP_SLOTS, 1.0, 0.0).astype(F32)
                parent = parents_ref[n, :, c].reshape(2 * lower_theta, lower_phi)
                wide = jnp.dot(parent, azimuth_ref[...], preferred_element_type=F32)
                wides.append((wide * used).astype(BF16))
                weights.append(jnp.where(slot == 1, 1.0, 0.0).astype(F32))
                turns.append(pl.ds(octant_ref[n] * ODD, top_theta))
            for tile in range(3):
                reals, imags = [], []
                for inner in range(2):
                    piece = wides[inner][:, tile * LANES : (tile + 1) * LANES]
                    piece = jnp.concatenate([piece[:lower_theta], piece[lower_theta:]], axis=1)
                    lifted = jnp.dot(theta_ref[...], piece, preferred_element_type=F32)
                    real, imag = lifted[:, :LANES], lifted[:, LANES:]
                    cosine = cos_ref[tile, turns[inner], :]
                    sine = sin_ref[tile, turns[inner], :]
                    reals.append(cosine * real - sine * imag)
                    imags.append(sine * real + cosine * imag)
                for part, (one, other) in enumerate((reals, imags)):
                    total_ref[tile, pl.ds(part * ODD, top_theta), :] += one + other
                    total_ref[tile, pl.ds((2 + part) * ODD, top_theta), :] += (
                        weights[0] * one + weights[1] * other
                    )
            return carry

        lax.fori_loop(0, parent_count // 2, two, 0)
        for tile in range(3):
            both = pl.ds(0, 2 * ODD)
            total_ref[tile, both, :] -= total_ref[tile, pl.ds(2 * ODD, 2 * ODD), :]

    def pack(c, to_x, to_rest):
        pair = to_x * 16 + to_rest // 2
        tiles = [
            total_ref[tile, pl.ds(pair * 3 + row, 4, stride=ODD), :]
            for row in range(3)
            for tile in range(3)
        ]
        line = jnp.concatenate(tiles, axis=1).astype(BF16)
        up_send[c, pair * 2, :, 0:BLOCK] = line[:, 0:BLOCK]
        up_send[c, pair * 2 + 1, :, 0:BLOCK] = line[:, BLOCK : 2 * BLOCK]

    rise(0)
    pl.semaphore_wait(barrier, count - 1)
    for c in range(COLUMNS):
        if c:
            rise(c)
        pack(c, x, y * 8 + z * 2)
        send_own(up_send.at[c], up_got.at[c], c)

        def pack_send(far, carry, c=c, first=0):
            for near in range(first, 4):
                pack(c, *chip(far, near))
                send_pair(up_send.at[c], up_got.at[c], far, near, c)
            return carry

        pack_send(0, 0, first=1)
        lax.fori_loop(1, pairs // 4, pack_send, 0, unroll=3)

    for load in loads[2:]:
        load.wait()

    def arrange(group):
        block = translators_ref[pl.ds(group * 4, 4)].reshape(8, BLOCK)
        for k in range(8):
            trans_ref[pl.ds(group * 72 + k, 8, stride=9), 0:72] = block[:, 72 * k : 72 * k + 72]

    def arrange_four(step, carry):
        for inner in range(4):
            arrange(step * 4 + inner)
        return carry

    lax.fori_loop(0, kinds // 16, arrange_four, 0)
    for group in range(kinds // 16 * 4, kinds // 4):
        arrange(group)
    slots = place_ref.shape[1]

    def select(shape, test):
        row = lax.broadcasted_iota(jnp.int32, shape, 0)
        column = lax.broadcasted_iota(jnp.int32, shape, 1)
        return jnp.where(test(row, column), 1.0, 0.0).astype(BF16)

    hot = select((boxes, slots), lambda row, column: row == place_ref[...])
    wider = select((slots, slots * 2), lambda row, column: row == column // 2)
    taller = select((boxes * 2, boxes), lambda row, column: row // 2 == column)
    hot = jnp.dot(hot, wider, preferred_element_type=F32).astype(BF16)
    hot = jnp.dot(taller, hot, preferred_element_type=F32)
    row = lax.broadcasted_iota(jnp.int32, hot.shape, 0)
    column = lax.broadcasted_iota(jnp.int32, hot.shape, 1)
    hot = jnp.where(lax.rem(row, 2) == lax.rem(column, 2), hot, 0.0)
    up_hot[...] = hot.astype(BF16)
    down_hot[...] = hot.T.astype(BF16)
    theta_flip[...] = theta_ref[...].astype(F32).T.astype(BF16)

    for c in range(COLUMNS):
        await_got(up_send.at[c], up_got.at[c], c)
        for tile in range(5):
            lanes = slice(tile * LANES, (tile + 1) * LANES)
            piece = up_got[c, :, :, lanes].reshape(count * 4, LANES)
            top = jnp.dot(up_hot[...], piece, preferred_element_type=F32)
            flat_ref[:, lanes] = top.astype(BF16).astype(F32)

        def spread(step, carry):
            for inner in range(4):
                group = step * 4 + inner
                block = flat_ref[pl.ds(pl.multiple_of(group * 8, 8), 8), :]
                for k in range(8):
                    field_ref[pl.ds(group * 72 + k, 8, stride=9), :] = block[
                        :, 72 * k : 72 * k + LANES
                    ]
            return carry

        lax.fori_loop(0, boxes // 16, spread, 0)

        def box(b):
            sums = [jnp.zeros((8, LANES), F32)] * 4
            for spot in range(far_count):
                source = source_ref[spot, b]
                kind = kind_ref[spot, b]
                trans_real = trans_ref[pl.ds(kind, 8), :]
                trans_imag = trans_ref[pl.ds(kind + 9, 8), :]
                real = field_ref[pl.ds(source, 8), :]
                imag = field_ref[pl.ds(source + 9, 8), :]
                sums[0] += trans_real * real
                sums[1] += trans_imag * imag
                sums[2] += trans_real * imag
                sums[3] += trans_imag * real
            done_ref[pl.ds(b * 18, 8), :] = sums[0] - sums[1]
            done_ref[pl.ds(b * 18 + 9, 8), :] = sums[2] + sums[3]

        def plain(step, carry):
            for inner in range(4):
                box(step * 4 + inner)
            return carry

        if c == 0:
            lax.fori_loop(0, boxes // 4, plain, 0)
        else:
            send_own(down_send.at[0], down_got.at[0], 2)

            def box_send(step, carry, first=0):
                for inner in range(4):
                    for near in range(inner % 2 * 2, inner % 2 * 2 + 2):
                        if inner // 2 * 4 + near >= first:
                            far = step * 2 + inner // 2
                            send_pair(down_send.at[0], down_got.at[0], far, near, 2)
                    box(step * 4 + inner)
                return carry

            box_send(0, 0, 1)
            lax.fori_loop(1, boxes // 8, box_send, 0)
            lax.fori_loop(boxes // 8, boxes // 4, plain, 0)

        def gather(step, carry):
            for inner in range(4):
                group = step * 4 + inner
                pieces = [
                    done_ref[pl.ds(group * 72 + k, 8, stride=9), :][:, 0:72] for k in range(8)
                ]
                pieces.append(jnp.zeros((8, 64), F32))
                rows = pl.ds(pl.multiple_of(group * 8, 8), 8)
                flat_ref[rows, :] = jnp.concatenate(pieces, axis=1)
            return carry

        lax.fori_loop(0, boxes // 16, gather, 0)
        for tile in range(5):
            lanes = slice(tile * LANES, (tile + 1) * LANES)
            piece = flat_ref[:, lanes].astype(BF16)
            out = jnp.dot(down_hot[...], piece, preferred_element_type=F32).astype(BF16)
            down_send[c, :, :, lanes] = out.reshape(count, 4, LANES)

    send_own(down_send.at[1], down_got.at[1], 3)

    def last_send(far, carry, first=0):
        for near in range(first, 4):
            send_pair(down_send.at[1], down_got.at[1], far, near, 3)
        return carry

    last_send(0, 0, first=1)
    lax.fori_loop(1, pairs // 4, last_send, 0)

    for c in range(COLUMNS):
        await_got(down_send.at[c], down_got.at[c], 2 + c)

        def unpack(step, carry, c=c):
            for inner in range(8):
                pair = step * 8 + inner
                line = jnp.concatenate(
                    [
                        down_got[c, pair * 2].astype(F32)[:, 0:BLOCK],
                        down_got[c, pair * 2 + 1].astype(F32)[:, 0:BLOCK],
                    ],
                    axis=1,
                )
                for row in range(3):
                    for tile in range(3):
                        at = (row * 3 + tile) * LANES
                        total_ref[tile, pl.ds(pair * 3 + row, 4, stride=ODD), :] = line[
                            :, at : at + LANES
                        ]
            return carry

        lax.fori_loop(0, pairs // 8, unpack, 0)

        def sink(n, carry, c=c):
            slot = slot_ref[n]
            target = jnp.minimum(slot, TOP_SLOTS - 1) * 2
            usable = jnp.where(slot < TOP_SLOTS, 1.0, 0.0).astype(F32)
            turn = pl.ds(octant_ref[n] * ODD, top_theta)
            for tile in range(3):
                cosine = cos_ref[tile, turn, :]
                sine = sin_ref[tile, turn, :]
                real = total_ref[tile, pl.ds(target * ODD, top_theta), :]
                imag = total_ref[tile, pl.ds((target + 1) * ODD, top_theta), :]
                turned = jnp.concatenate(
                    [
                        (cosine * real + sine * imag).astype(BF16),
                        (cosine * imag - sine * real).astype(BF16),
                    ],
                    axis=1,
                )
                narrowed = jnp.dot(theta_flip[...], turned, preferred_element_type=F32)
                narrowed = narrowed.astype(BF16)
                lanes = slice(tile * LANES, (tile + 1) * LANES)
                narrow_ref[:lower_theta, lanes] = narrowed[:, :LANES]
                narrow_ref[lower_theta:, lanes] = narrowed[:, LANES:]
            result = lax.dot_general(
                narrow_ref[...],
                azimuth_ref[...],
                (((1,), (1,)), ((), ())),
                preferred_element_type=F32,
            )
            out_ref[n, :, c] = (result * usable).astype(BF16).reshape(2, lower_theta, lower_phi)
            return carry

        lax.fori_loop(0, parent_count, sink, 0, unroll=2)

    for side, out in enumerate((up_send.at[0], up_send.at[1], down_send.at[0], down_send.at[1])):
        some = out.at[pl.ds(1, count - 1)]
        pltpu.make_async_copy(some, some, send_sem.at[side]).wait()


VMEM = pl.BlockSpec(memory_space=pltpu.VMEM)
SMEM = pl.BlockSpec(memory_space=pltpu.SMEM)
ANY = pl.BlockSpec(memory_space=pl.ANY)
LIMIT = 56 * 1024 * 1024


def shards(
    parents,
    theta_table,
    azimuth_table,
    phase_angle,
    translators,
    parent_slot,
    parent_octant,
    top_box,
    far_source,
    far_kind,
):
    top_theta, lower_theta = theta_table.shape
    devices = top_box.shape[0] // TOP_SLOTS
    boxes = far_source.shape[0]
    kinds = translators.shape[0]
    wire = pltpu.VMEM((COLUMNS, devices, 4, 640), BF16)
    rows = pltpu.VMEM((boxes * 18 + 8, LANES), F32)
    return pl.pallas_call(
        kernel,
        out_shape=jax.ShapeDtypeStruct(parents.shape, BF16),
        in_specs=[SMEM] * 2 + [VMEM] * 5 + [ANY] * 3,
        out_specs=VMEM,
        scratch_shapes=[
            pltpu.VMEM(phase_angle.shape, F32),
            pltpu.VMEM(parents.shape, BF16),
            pltpu.VMEM(translators.shape, F32),
            pltpu.VMEM((3, 8 * ODD + 8, LANES), F32),
            pltpu.VMEM((3, 8 * ODD + 8, LANES), F32),
            pltpu.VMEM((3, 4 * ODD + 4, LANES), F32),
            wire,
            wire,
            wire,
            wire,
            pltpu.VMEM((2,) + far_source.shape[::-1], jnp.int32),
            pltpu.SMEM(far_source.shape[::-1], jnp.int32),
            pltpu.SMEM(far_source.shape[::-1], jnp.int32),
            pltpu.VMEM((kinds * 18 + 8, LANES), F32),
            rows,
            rows,
            pltpu.VMEM((boxes * 2, 640), F32),
            pltpu.VMEM((boxes * 2, devices * 4), BF16),
            pltpu.VMEM((devices * 4, boxes * 2), BF16),
            pltpu.VMEM((lower_theta, top_theta), BF16),
            pltpu.VMEM((2 * lower_theta, azimuth_table.shape[1]), BF16),
            pltpu.SemaphoreType.DMA((5,)),
            pltpu.SemaphoreType.DMA((4,)),
            pltpu.SemaphoreType.DMA((4,)),
            pltpu.SemaphoreType.DMA((4,)),
        ],
        compiler_params=pltpu.CompilerParams(
            collective_id=0, has_side_effects=True, vmem_limit_bytes=LIMIT
        ),
    )(
        parent_slot,
        parent_octant,
        far_source.T,
        far_kind.T,
        top_box.reshape(1, -1),
        theta_table,
        azimuth_table,
        phase_angle,
        parents,
        translators,
    )


def solution(mesh):
    placed = (
        P(("grp", "dev"), None, None, None, None),
        P(),
        P(),
        P(),
        P(None, None, ("grp", "dev")),
        P(("grp", "dev")),
        P(("grp", "dev")),
        P(),
        P(),
        P(),
    )
    return jax.shard_map(
        shards,
        mesh=mesh,
        in_specs=placed,
        out_specs=P(("grp", "dev"), None, None, None, None),
        check_vma=False,
    )
```

```python
import jax
import jax.numpy as jnp
from jax import lax
from jax.experimental import pallas as pl
from jax.experimental.pallas import tpu as pltpu
from jax.sharding import PartitionSpec as P

MESH = pl.DeviceIdType.MESH
F32 = jnp.float32
BF16 = jnp.bfloat16
TOP_SLOTS = 2
LANES = 128
SINE_TERMS = (
    0.9999999957103306,
    -0.16666657960973935,
    0.00833305040018596,
    -0.00019809029932038968,
    2.6051282412897536e-06,
)
COSINE_TERMS = (
    0.9999999531875788,
    -0.49999904965506836,
    0.04166357656486354,
    -0.0013853649037081687,
    2.315275975496213e-05,
)


def horner(terms, z):
    total = terms[-1] * z + terms[-2]
    for term in terms[-3::-1]:
        total = total * z + term
    return total


BLOCK = 576
ODD = 193
COLUMNS = 2


def kernel(
    slot_ref, octant_ref, source_in, kind_in, place_ref, theta_ref, azimuth_ref,
    phase_hbm, parents_hbm, translators_hbm,
    out_ref,
    phase_ref, parents_ref, translators_ref, cos_ref, sin_ref, total_ref,
    up_send, up_got, down_send, down_got,
    scaled_ref, source_ref, kind_ref, trans_ref, field_ref, done_ref, flat_ref, up_hot, down_hot, theta_flip, narrow_ref,
    in_sem, own_sem, send_sem, got_sem,
):
    top_theta, lower_theta = theta_ref.shape
    lower_phi = azimuth_ref.shape[0]
    count = up_send.shape[1]
    pairs = count // 2
    parent_count = out_ref.shape[0]
    far_count, boxes = source_in.shape
    kinds = translators_ref.shape[0]

    x = lax.axis_index("grp")
    rest = lax.axis_index("dev")
    y, z, core = rest // 8, lax.rem(rest, 8) // 2, lax.rem(rest, 2)
    me = x * 32 + rest

    turn_x = [lax.rem(x + near, 4) for near in range(4)]

    def chip(far, near):
        to_y = lax.rem(y + near + far // 4, 4)
        to_z = lax.rem(z + near + lax.rem(far, 4), 4)
        return turn_x[near], to_y * 8 + to_z * 2

    loads = [
        pltpu.make_async_copy(phase_hbm, phase_ref, in_sem.at[0]),
        pltpu.make_async_copy(parents_hbm, parents_ref, in_sem.at[1]),
        pltpu.make_async_copy(translators_hbm, translators_ref, in_sem.at[2]),
    ]
    for load in loads:
        load.start()

    scaled_ref[0] = source_in[...] * 18
    scaled_ref[1] = kind_in[...] * 18
    loads.append(pltpu.make_async_copy(scaled_ref.at[0], source_ref, in_sem.at[3]))
    loads.append(pltpu.make_async_copy(scaled_ref.at[1], kind_ref, in_sem.at[4]))
    for load in loads[3:]:
        load.start()

    barrier = pltpu.get_barrier_semaphore()

    def greet(far, near):
        to_x, to_rest = chip(far, near)
        for to_core in range(2):
            pl.semaphore_signal(
                barrier, inc=1, device_id=(to_x, to_rest + to_core), device_id_type=MESH
            )

    pl.semaphore_signal(barrier, inc=1, device_id=(x, rest + 1 - 2 * core), device_id_type=MESH)
    loads[0].wait()

    def fill(row):
        for tile in range(3):
            place = pl.ds(pl.multiple_of(row * 384 + tile * LANES, LANES), LANES)
            half = phase_ref[:, place] * 0.5
            square = half * half
            sine = horner(SINE_TERMS, square) * half
            cosine = horner(COSINE_TERMS, square)
            rows = pl.ds(row, 8, stride=ODD)
            sin_ref[tile, rows, :] = 2.0 * sine * cosine
            cos_ref[tile, rows, :] = 1.0 - 2.0 * sine * sine

    def fill_greet(far, carry, first=0):
        for inner in range(12):
            fill(far * 12 + inner)
        for near in range(first, 4):
            greet(far, near)
        return carry

    fill_greet(0, 0, 1)
    lax.fori_loop(1, pairs // 4, fill_greet, 0)
    loads[1].wait()

    def send(out, got, block, device, side):
        pltpu.make_async_remote_copy(
            src_ref=out.at[block],
            dst_ref=got.at[me],
            send_sem=send_sem.at[side],
            recv_sem=got_sem.at[side],
            device_id=device,
            device_id_type=MESH,
        ).start()

    def send_pair(out, got, far, near, side):
        to_x, to_rest = chip(far, near)
        for to_core in range(2):
            device = (to_x, to_rest + to_core)
            send(out, got, to_x * 32 + to_rest + to_core, device, side)

    def send_own(out, got, side):
        send(out, got, me + 1 - 2 * core, (x, rest + 1 - 2 * core), side)
        pltpu.make_async_copy(out.at[me], got.at[me], own_sem.at[side]).start()

    def await_got(out, got, side):
        pltpu.make_async_copy(out.at[me], got.at[me], own_sem.at[side]).wait()
        some = got.at[pl.ds(1, count - 1)]
        pltpu.make_async_copy(some, some, got_sem.at[side]).wait()

    def rise(c):
        total_ref[...] = jnp.zeros_like(total_ref)

        def two(step, carry, first=0):
            if c == 1:
                spots = [(step * 4 + far, near) for far in range(4) for near in range(4)]
                for far, near in spots[first:]:
                    send_pair(up_send.at[0], up_got.at[0], far, near, 0)
            wides, weights, turns = [], [], []
            for inner in range(2):
                n = step * 2 + inner
                slot = slot_ref[n]
                used = jnp.where(slot < TOP_SLOTS, 1.0, 0.0).astype(F32)
                parent = parents_ref[n, :, c].reshape(2 * lower_theta, lower_phi)
                wide = jnp.dot(parent, azimuth_ref[...], preferred_element_type=F32)
                wides.append((wide * used).astype(BF16))
                weights.append(jnp.where(slot == 1, 1.0, 0.0).astype(F32))
                turns.append(pl.ds(octant_ref[n] * ODD, top_theta))
            for tile in range(3):
                reals, imags = [], []
                for inner in range(2):
                    piece = wides[inner][:, tile * LANES : (tile + 1) * LANES]
                    piece = jnp.concatenate([piece[:lower_theta], piece[lower_theta:]], axis=1)
                    lifted = jnp.dot(theta_ref[...], piece, preferred_element_type=F32)
                    real, imag = lifted[:, :LANES], lifted[:, LANES:]
                    cosine = cos_ref[tile, turns[inner], :]
                    sine = sin_ref[tile, turns[inner], :]
                    reals.append(cosine * real - sine * imag)
                    imags.append(sine * real + cosine * imag)
                for part, (one, other) in enumerate((reals, imags)):
                    total_ref[tile, pl.ds(part * ODD, top_theta), :] += one + other
                    total_ref[tile, pl.ds((2 + part) * ODD, top_theta), :] += (
                        weights[0] * one + weights[1] * other
                    )
            return carry

        if c == 1:
            two(0, 0, first=1)
            lax.fori_loop(1, parent_count // 2, two, 0)
        else:
            lax.fori_loop(0, parent_count // 2, two, 0)
        for tile in range(3):
            both = pl.ds(0, 2 * ODD)
            total_ref[tile, both, :] -= total_ref[tile, pl.ds(2 * ODD, 2 * ODD), :]

    def pack(c, to_x, to_rest):
        pair = to_x * 16 + to_rest // 2
        tiles = [
            total_ref[tile, pl.ds(pair * 3 + row, 4, stride=ODD), :]
            for row in range(3)
            for tile in range(3)
        ]
        line = jnp.concatenate(tiles, axis=1).astype(BF16)
        up_send[c, pair * 2, :, 0:BLOCK] = line[:, 0:BLOCK]
        up_send[c, pair * 2 + 1, :, 0:BLOCK] = line[:, BLOCK : 2 * BLOCK]

    rise(0)
    pl.semaphore_wait(barrier, count - 1)
    for c in range(COLUMNS):
        if c:
            rise(c)
        pack(c, x, y * 8 + z * 2)
        send_own(up_send.at[c], up_got.at[c], c)

        def pack_send(step, carry, c=c, first=0):
            spots = [(step * 4 + far, near) for far in range(4) for near in range(4)][first:]
            for far, near in spots:
                pack(c, *chip(far, near))
            if c == 1:
                for far, near in spots:
                    send_pair(up_send.at[c], up_got.at[c], far, near, c)
            return carry

        pack_send(0, 0, first=1)
        lax.fori_loop(1, pairs // 16, pack_send, 0)

    for load in loads[2:]:
        load.wait()

    def arrange(group):
        block = translators_ref[pl.ds(group * 4, 4)].reshape(8, BLOCK)
        for k in range(8):
            trans_ref[pl.ds(group * 72 + k, 8, stride=9), 0:72] = block[:, 72 * k : 72 * k + 72]

    def arrange_four(step, carry):
        for inner in range(4):
            arrange(step * 4 + inner)
        return carry

    lax.fori_loop(0, kinds // 16, arrange_four, 0)
    for group in range(kinds // 16 * 4, kinds // 4):
        arrange(group)
    slots = place_ref.shape[1]

    def select(shape, test):
        row = lax.broadcasted_iota(jnp.int32, shape, 0)
        column = lax.broadcasted_iota(jnp.int32, shape, 1)
        return jnp.where(test(row, column), 1.0, 0.0).astype(BF16)

    hot = select((boxes, slots), lambda row, column: row == place_ref[...])
    wider = select((slots, slots * 2), lambda row, column: row == column // 2)
    taller = select((boxes * 2, boxes), lambda row, column: row // 2 == column)
    hot = jnp.dot(hot, wider, preferred_element_type=F32).astype(BF16)
    hot = jnp.dot(taller, hot, preferred_element_type=F32)
    row = lax.broadcasted_iota(jnp.int32, hot.shape, 0)
    column = lax.broadcasted_iota(jnp.int32, hot.shape, 1)
    hot = jnp.where(lax.rem(row, 2) == lax.rem(column, 2), hot, 0.0)
    up_hot[...] = hot.astype(BF16)
    down_hot[...] = hot.T.astype(BF16)
    theta_flip[...] = theta_ref[...].astype(F32).T.astype(BF16)

    for c in range(COLUMNS):
        await_got(up_send.at[c], up_got.at[c], c)
        for tile in range(5):
            lanes = slice(tile * LANES, (tile + 1) * LANES)
            piece = up_got[c, :, :, lanes].reshape(count * 4, LANES)
            top = jnp.dot(up_hot[...], piece, preferred_element_type=F32)
            flat_ref[:, lanes] = top.astype(BF16).astype(F32)

        def spread(step, carry):
            for inner in range(4):
                group = step * 4 + inner
                block = flat_ref[pl.ds(pl.multiple_of(group * 8, 8), 8), :]
                for k in range(8):
                    field_ref[pl.ds(group * 72 + k, 8, stride=9), :] = block[
                        :, 72 * k : 72 * k + LANES
                    ]
            return carry

        lax.fori_loop(0, boxes // 16, spread, 0)

        def box(b):
            sums = [jnp.zeros((8, LANES), F32)] * 4
            for spot in range(far_count):
                source = source_ref[spot, b]
                kind = kind_ref[spot, b]
                trans_real = trans_ref[pl.ds(kind, 8), :]
                trans_imag = trans_ref[pl.ds(kind + 9, 8), :]
                real = field_ref[pl.ds(source, 8), :]
                imag = field_ref[pl.ds(source + 9, 8), :]
                sums[0] += trans_real * real
                sums[1] += trans_imag * imag
                sums[2] += trans_real * imag
                sums[3] += trans_imag * real
            done_ref[pl.ds(b * 18, 8), :] = sums[0] - sums[1]
            done_ref[pl.ds(b * 18 + 9, 8), :] = sums[2] + sums[3]

        def plain(step, carry):
            for inner in range(4):
                box(step * 4 + inner)
            return carry

        if c == 0:
            lax.fori_loop(0, boxes // 4, plain, 0)
        else:
            lax.fori_loop(0, boxes // 4, plain, 0)

        def gather(step, carry):
            for inner in range(4):
                group = step * 4 + inner
                pieces = [
                    done_ref[pl.ds(group * 72 + k, 8, stride=9), :][:, 0:72] for k in range(8)
                ]
                pieces.append(jnp.zeros((8, 64), F32))
                rows = pl.ds(pl.multiple_of(group * 8, 8), 8)
                flat_ref[rows, :] = jnp.concatenate(pieces, axis=1)
            return carry

        lax.fori_loop(0, boxes // 16, gather, 0)
        for tile in range(5):
            lanes = slice(tile * LANES, (tile + 1) * LANES)
            piece = flat_ref[:, lanes].astype(BF16)
            out = jnp.dot(down_hot[...], piece, preferred_element_type=F32).astype(BF16)
            down_send[c, :, :, lanes] = out.reshape(count, 4, LANES)
        send_own(down_send.at[c], down_got.at[c], 2 + c)

        def back_send(far, carry, c=c, first=0):
            for near in range(first, 4):
                send_pair(down_send.at[c], down_got.at[c], far, near, 2 + c)
            return carry

        back_send(0, 0, first=1)
        lax.fori_loop(1, pairs // 4, back_send, 0)

    for c in range(COLUMNS):
        await_got(down_send.at[c], down_got.at[c], 2 + c)

        def unpack(step, carry, c=c):
            for inner in range(8):
                pair = step * 8 + inner
                line = jnp.concatenate(
                    [
                        down_got[c, pair * 2].astype(F32)[:, 0:BLOCK],
                        down_got[c, pair * 2 + 1].astype(F32)[:, 0:BLOCK],
                    ],
                    axis=1,
                )
                for row in range(3):
                    for tile in range(3):
                        at = (row * 3 + tile) * LANES
                        total_ref[tile, pl.ds(pair * 3 + row, 4, stride=ODD), :] = line[
                            :, at : at + LANES
                        ]
            return carry

        lax.fori_loop(0, pairs // 8, unpack, 0)

        def sink(n, carry, c=c):
            slot = slot_ref[n]
            target = jnp.minimum(slot, TOP_SLOTS - 1) * 2
            usable = jnp.where(slot < TOP_SLOTS, 1.0, 0.0).astype(F32)
            turn = pl.ds(octant_ref[n] * ODD, top_theta)
            for tile in range(3):
                cosine = cos_ref[tile, turn, :]
                sine = sin_ref[tile, turn, :]
                real = total_ref[tile, pl.ds(target * ODD, top_theta), :]
                imag = total_ref[tile, pl.ds((target + 1) * ODD, top_theta), :]
                turned = jnp.concatenate(
                    [
                        (cosine * real + sine * imag).astype(BF16),
                        (cosine * imag - sine * real).astype(BF16),
                    ],
                    axis=1,
                )
                narrowed = jnp.dot(theta_flip[...], turned, preferred_element_type=F32)
                narrowed = narrowed.astype(BF16)
                lanes = slice(tile * LANES, (tile + 1) * LANES)
                narrow_ref[:lower_theta, lanes] = narrowed[:, :LANES]
                narrow_ref[lower_theta:, lanes] = narrowed[:, LANES:]
            result = lax.dot_general(
                narrow_ref[...],
                azimuth_ref[...],
                (((1,), (1,)), ((), ())),
                preferred_element_type=F32,
            )
            out_ref[n, :, c] = (result * usable).astype(BF16).reshape(2, lower_theta, lower_phi)
            return carry

        lax.fori_loop(0, parent_count, sink, 0, unroll=2)

    for side, out in enumerate((up_send.at[0], up_send.at[1], down_send.at[0], down_send.at[1])):
        some = out.at[pl.ds(1, count - 1)]
        pltpu.make_async_copy(some, some, send_sem.at[side]).wait()


VMEM = pl.BlockSpec(memory_space=pltpu.VMEM)
SMEM = pl.BlockSpec(memory_space=pltpu.SMEM)
ANY = pl.BlockSpec(memory_space=pl.ANY)
LIMIT = 56 * 1024 * 1024


def shards(
    parents,
    theta_table,
    azimuth_table,
    phase_angle,
    translators,
    parent_slot,
    parent_octant,
    top_box,
    far_source,
    far_kind,
):
    top_theta, lower_theta = theta_table.shape
    devices = top_box.shape[0] // TOP_SLOTS
    boxes = far_source.shape[0]
    kinds = translators.shape[0]
    wire = pltpu.VMEM((COLUMNS, devices, 4, 640), BF16)
    rows = pltpu.VMEM((boxes * 18 + 8, LANES), F32)
    return pl.pallas_call(
        kernel,
        out_shape=jax.ShapeDtypeStruct(parents.shape, BF16),
        in_specs=[SMEM] * 2 + [VMEM] * 5 + [ANY] * 3,
        out_specs=VMEM,
        scratch_shapes=[
            pltpu.VMEM(phase_angle.shape, F32),
            pltpu.VMEM(parents.shape, BF16),
            pltpu.VMEM(translators.shape, F32),
            pltpu.VMEM((3, 8 * ODD + 8, LANES), F32),
            pltpu.VMEM((3, 8 * ODD + 8, LANES), F32),
            pltpu.VMEM((3, 4 * ODD + 4, LANES), F32),
            wire,
            wire,
            wire,
            wire,
            pltpu.VMEM((2,) + far_source.shape[::-1], jnp.int32),
            pltpu.SMEM(far_source.shape[::-1], jnp.int32),
            pltpu.SMEM(far_source.shape[::-1], jnp.int32),
            pltpu.VMEM((kinds * 18 + 8, LANES), F32),
            rows,
            rows,
            pltpu.VMEM((boxes * 2, 640), F32),
            pltpu.VMEM((boxes * 2, devices * 4), BF16),
            pltpu.VMEM((devices * 4, boxes * 2), BF16),
            pltpu.VMEM((lower_theta, top_theta), BF16),
            pltpu.VMEM((2 * lower_theta, azimuth_table.shape[1]), BF16),
            pltpu.SemaphoreType.DMA((5,)),
            pltpu.SemaphoreType.DMA((4,)),
            pltpu.SemaphoreType.DMA((4,)),
            pltpu.SemaphoreType.DMA((4,)),
        ],
        compiler_params=pltpu.CompilerParams(
            collective_id=0, has_side_effects=True, vmem_limit_bytes=LIMIT
        ),
    )(
        parent_slot,
        parent_octant,
        far_source.T,
        far_kind.T,
        top_box.reshape(1, -1),
        theta_table,
        azimuth_table,
        phase_angle,
        parents,
        translators,
    )


def solution(mesh):
    placed = (
        P(("grp", "dev"), None, None, None, None),
        P(),
        P(),
        P(),
        P(None, None, ("grp", "dev")),
        P(("grp", "dev")),
        P(("grp", "dev")),
        P(),
        P(),
        P(),
    )
    return jax.shard_map(
        shards,
        mesh=mesh,
        in_specs=placed,
        out_specs=P(("grp", "dev"), None, None, None, None),
        check_vma=False,
    )
```

```python
import jax
import jax.numpy as jnp
from jax import lax
from jax.experimental import pallas as pl
from jax.experimental.pallas import tpu as pltpu
from jax.sharding import PartitionSpec as P

MESH = pl.DeviceIdType.MESH
F32 = jnp.float32
BF16 = jnp.bfloat16
TOP_SLOTS = 2
LANES = 128
SINE_TERMS = (
    0.9999999957103306,
    -0.16666657960973935,
    0.00833305040018596,
    -0.00019809029932038968,
    2.6051282412897536e-06,
)
COSINE_TERMS = (
    0.9999999531875788,
    -0.49999904965506836,
    0.04166357656486354,
    -0.0013853649037081687,
    2.315275975496213e-05,
)


def horner(terms, z):
    total = terms[-1] * z + terms[-2]
    for term in terms[-3::-1]:
        total = total * z + term
    return total


BLOCK = 576
ODD = 193
COLUMNS = 2


def kernel(
    slot_ref, octant_ref, source_in, kind_in, place_ref, theta_ref, azimuth_ref,
    phase_hbm, parents_hbm, translators_hbm,
    out_ref,
    phase_ref, parents_ref, translators_ref, cos_ref, sin_ref, total_ref,
    up_send, up_got, down_send, down_got,
    scaled_ref, source_ref, kind_ref, trans_ref, field_ref, done_ref, flat_ref, up_hot, down_hot, theta_flip, narrow_ref,
    in_sem, own_sem, send_sem, got_sem,
):
    top_theta, lower_theta = theta_ref.shape
    lower_phi = azimuth_ref.shape[0]
    count = up_send.shape[1]
    pairs = count // 2
    parent_count = out_ref.shape[0]
    far_count, boxes = source_in.shape
    kinds = translators_ref.shape[0]

    x = lax.axis_index("grp")
    rest = lax.axis_index("dev")
    y, z, core = rest // 8, lax.rem(rest, 8) // 2, lax.rem(rest, 2)
    me = x * 32 + rest

    turn_x = [lax.rem(x + near, 4) for near in range(4)]

    def chip(far, near):
        to_y = lax.rem(y + near + far // 4, 4)
        to_z = lax.rem(z + near + lax.rem(far, 4), 4)
        return turn_x[near], to_y * 8 + to_z * 2

    loads = [
        pltpu.make_async_copy(phase_hbm, phase_ref, in_sem.at[0]),
        pltpu.make_async_copy(parents_hbm, parents_ref, in_sem.at[1]),
        pltpu.make_async_copy(translators_hbm, translators_ref, in_sem.at[2]),
    ]
    for load in loads:
        load.start()

    scaled_ref[0] = source_in[...] * 18
    scaled_ref[1] = kind_in[...] * 18
    loads.append(pltpu.make_async_copy(scaled_ref.at[0], source_ref, in_sem.at[3]))
    loads.append(pltpu.make_async_copy(scaled_ref.at[1], kind_ref, in_sem.at[4]))
    for load in loads[3:]:
        load.start()

    barrier = pltpu.get_barrier_semaphore()

    def greet(far, near):
        to_x, to_rest = chip(far, near)
        for to_core in range(2):
            pl.semaphore_signal(
                barrier, inc=1, device_id=(to_x, to_rest + to_core), device_id_type=MESH
            )

    pl.semaphore_signal(barrier, inc=1, device_id=(x, rest + 1 - 2 * core), device_id_type=MESH)

    def greet_only(far, carry, first=0):
        for near in range(first, 4):
            greet(far, near)
        return carry

    greet_only(0, 0, 1)
    lax.fori_loop(1, 4, greet_only, 0)
    loads[0].wait()

    def fill(row):
        for tile in range(3):
            place = pl.ds(pl.multiple_of(row * 384 + tile * LANES, LANES), LANES)
            half = phase_ref[:, place] * 0.5
            square = half * half
            sine = horner(SINE_TERMS, square) * half
            cosine = horner(COSINE_TERMS, square)
            rows = pl.ds(row, 8, stride=ODD)
            sin_ref[tile, rows, :] = 2.0 * sine * cosine
            cos_ref[tile, rows, :] = 1.0 - 2.0 * sine * sine

    def fill_only(step, carry):
        for inner in range(12):
            fill(step * 12 + inner)
        return carry

    def fill_greet(far, carry):
        fill_only(far, carry)
        return greet_only(far, carry)

    lax.fori_loop(0, 4, fill_only, 0)
    lax.fori_loop(4, pairs // 4, fill_greet, 0)
    loads[1].wait()

    def send(out, got, block, device, side):
        pltpu.make_async_remote_copy(
            src_ref=out.at[block],
            dst_ref=got.at[me],
            send_sem=send_sem.at[side],
            recv_sem=got_sem.at[side],
            device_id=device,
            device_id_type=MESH,
        ).start()

    def send_pair(out, got, far, near, side):
        to_x, to_rest = chip(far, near)
        for to_core in range(2):
            device = (to_x, to_rest + to_core)
            send(out, got, to_x * 32 + to_rest + to_core, device, side)

    def send_own(out, got, side):
        send(out, got, me + 1 - 2 * core, (x, rest + 1 - 2 * core), side)
        pltpu.make_async_copy(out.at[me], got.at[me], own_sem.at[side]).start()

    def await_got(out, got, side):
        pltpu.make_async_copy(out.at[me], got.at[me], own_sem.at[side]).wait()
        some = got.at[pl.ds(1, count - 1)]
        pltpu.make_async_copy(some, some, got_sem.at[side]).wait()

    def rise(c):
        total_ref[...] = jnp.zeros_like(total_ref)

        def two(step, carry, first=0):
            if c == 1:
                spots = [(step * 4 + far, near) for far in range(4) for near in range(4)]
                for far, near in spots[first:]:
                    send_pair(up_send.at[0], up_got.at[0], far, near, 0)
            wides, weights, turns = [], [], []
            for inner in range(2):
                n = step * 2 + inner
                slot = slot_ref[n]
                used = jnp.where(slot < TOP_SLOTS, 1.0, 0.0).astype(F32)
                parent = parents_ref[n, :, c].reshape(2 * lower_theta, lower_phi)
                wide = jnp.dot(parent, azimuth_ref[...], preferred_element_type=F32)
                wides.append((wide * used).astype(BF16))
                weights.append(jnp.where(slot == 1, 1.0, 0.0).astype(F32))
                turns.append(pl.ds(octant_ref[n] * ODD, top_theta))
            for tile in range(3):
                reals, imags = [], []
                for inner in range(2):
                    piece = wides[inner][:, tile * LANES : (tile + 1) * LANES]
                    piece = jnp.concatenate([piece[:lower_theta], piece[lower_theta:]], axis=1)
                    lifted = jnp.dot(theta_ref[...], piece, preferred_element_type=F32)
                    real, imag = lifted[:, :LANES], lifted[:, LANES:]
                    cosine = cos_ref[tile, turns[inner], :]
                    sine = sin_ref[tile, turns[inner], :]
                    reals.append(cosine * real - sine * imag)
                    imags.append(sine * real + cosine * imag)
                for part, (one, other) in enumerate((reals, imags)):
                    total_ref[tile, pl.ds(part * ODD, top_theta), :] += one + other
                    total_ref[tile, pl.ds((2 + part) * ODD, top_theta), :] += (
                        weights[0] * one + weights[1] * other
                    )
            return carry

        if c == 1:
            two(0, 0, first=1)
            lax.fori_loop(1, parent_count // 2, two, 0)
        else:
            lax.fori_loop(0, parent_count // 2, two, 0)
        for tile in range(3):
            both = pl.ds(0, 2 * ODD)
            total_ref[tile, both, :] -= total_ref[tile, pl.ds(2 * ODD, 2 * ODD), :]

    def pack(c, to_x, to_rest):
        pair = to_x * 16 + to_rest // 2
        tiles = [
            total_ref[tile, pl.ds(pair * 3 + row, 4, stride=ODD), :]
            for row in range(3)
            for tile in range(3)
        ]
        line = jnp.concatenate(tiles, axis=1).astype(BF16)
        up_send[c, pair * 2, :, 0:BLOCK] = line[:, 0:BLOCK]
        up_send[c, pair * 2 + 1, :, 0:BLOCK] = line[:, BLOCK : 2 * BLOCK]

    rise(0)
    pl.semaphore_wait(barrier, count - 1)
    for c in range(COLUMNS):
        if c:
            rise(c)
        pack(c, x, y * 8 + z * 2)
        send_own(up_send.at[c], up_got.at[c], c)

        def pack_send(step, carry, c=c, first=0):
            spots = [(step * 4 + far, near) for far in range(4) for near in range(4)][first:]
            for far, near in spots:
                pack(c, *chip(far, near))
            if c == 1:
                for far, near in spots:
                    send_pair(up_send.at[c], up_got.at[c], far, near, c)
            return carry

        pack_send(0, 0, first=1)
        lax.fori_loop(1, pairs // 16, pack_send, 0)

    for load in loads[2:]:
        load.wait()

    def arrange(group):
        block = translators_ref[pl.ds(group * 4, 4)].reshape(8, BLOCK)
        for k in range(8):
            trans_ref[pl.ds(group * 72 + k, 8, stride=9), 0:72] = block[:, 72 * k : 72 * k + 72]

    def arrange_four(step, carry):
        for inner in range(4):
            arrange(step * 4 + inner)
        return carry

    lax.fori_loop(0, kinds // 16, arrange_four, 0)
    for group in range(kinds // 16 * 4, kinds // 4):
        arrange(group)
    slots = place_ref.shape[1]

    def select(shape, test):
        row = lax.broadcasted_iota(jnp.int32, shape, 0)
        column = lax.broadcasted_iota(jnp.int32, shape, 1)
        return jnp.where(test(row, column), 1.0, 0.0).astype(BF16)

    hot = select((boxes, slots), lambda row, column: row == place_ref[...])
    wider = select((slots, slots * 2), lambda row, column: row == column // 2)
    taller = select((boxes * 2, boxes), lambda row, column: row // 2 == column)
    hot = jnp.dot(hot, wider, preferred_element_type=F32).astype(BF16)
    hot = jnp.dot(taller, hot, preferred_element_type=F32)
    row = lax.broadcasted_iota(jnp.int32, hot.shape, 0)
    column = lax.broadcasted_iota(jnp.int32, hot.shape, 1)
    hot = jnp.where(lax.rem(row, 2) == lax.rem(column, 2), hot, 0.0)
    up_hot[...] = hot.astype(BF16)
    down_hot[...] = hot.T.astype(BF16)
    theta_flip[...] = theta_ref[...].astype(F32).T.astype(BF16)

    for c in range(COLUMNS):
        await_got(up_send.at[c], up_got.at[c], c)
        for tile in range(5):
            lanes = slice(tile * LANES, (tile + 1) * LANES)
            piece = up_got[c, :, :, lanes].reshape(count * 4, LANES)
            top = jnp.dot(up_hot[...], piece, preferred_element_type=F32)
            flat_ref[:, lanes] = top.astype(BF16).astype(F32)

        def spread(step, carry):
            for inner in range(4):
                group = step * 4 + inner
                block = flat_ref[pl.ds(pl.multiple_of(group * 8, 8), 8), :]
                for k in range(8):
                    field_ref[pl.ds(group * 72 + k, 8, stride=9), :] = block[
                        :, 72 * k : 72 * k + LANES
                    ]
            return carry

        lax.fori_loop(0, boxes // 16, spread, 0)

        def box(b):
            sums = [jnp.zeros((8, LANES), F32)] * 4
            for spot in range(far_count):
                source = source_ref[spot, b]
                kind = kind_ref[spot, b]
                trans_real = trans_ref[pl.ds(kind, 8), :]
                trans_imag = trans_ref[pl.ds(kind + 9, 8), :]
                real = field_ref[pl.ds(source, 8), :]
                imag = field_ref[pl.ds(source + 9, 8), :]
                sums[0] += trans_real * real
                sums[1] += trans_imag * imag
                sums[2] += trans_real * imag
                sums[3] += trans_imag * real
            done_ref[pl.ds(b * 18, 8), :] = sums[0] - sums[1]
            done_ref[pl.ds(b * 18 + 9, 8), :] = sums[2] + sums[3]

        def plain(step, carry):
            for inner in range(4):
                box(step * 4 + inner)
            return carry

        if c == 0:
            lax.fori_loop(0, boxes // 4, plain, 0)
        else:
            lax.fori_loop(0, boxes // 4, plain, 0)

        def gather(step, carry):
            for inner in range(4):
                group = step * 4 + inner
                pieces = [
                    done_ref[pl.ds(group * 72 + k, 8, stride=9), :][:, 0:72] for k in range(8)
                ]
                pieces.append(jnp.zeros((8, 64), F32))
                rows = pl.ds(pl.multiple_of(group * 8, 8), 8)
                flat_ref[rows, :] = jnp.concatenate(pieces, axis=1)
            return carry

        lax.fori_loop(0, boxes // 16, gather, 0)
        for tile in range(5):
            lanes = slice(tile * LANES, (tile + 1) * LANES)
            piece = flat_ref[:, lanes].astype(BF16)
            out = jnp.dot(down_hot[...], piece, preferred_element_type=F32).astype(BF16)
            down_send[c, :, :, lanes] = out.reshape(count, 4, LANES)
        send_own(down_send.at[c], down_got.at[c], 2 + c)

        def back_send(far, carry, c=c, first=0):
            for near in range(first, 4):
                send_pair(down_send.at[c], down_got.at[c], far, near, 2 + c)
            return carry

        back_send(0, 0, first=1)
        lax.fori_loop(1, pairs // 4, back_send, 0)

    for c in range(COLUMNS):
        await_got(down_send.at[c], down_got.at[c], 2 + c)

        def unpack(step, carry, c=c):
            for inner in range(8):
                pair = step * 8 + inner
                line = jnp.concatenate(
                    [
                        down_got[c, pair * 2].astype(F32)[:, 0:BLOCK],
                        down_got[c, pair * 2 + 1].astype(F32)[:, 0:BLOCK],
                    ],
                    axis=1,
                )
                for row in range(3):
                    for tile in range(3):
                        at = (row * 3 + tile) * LANES
                        total_ref[tile, pl.ds(pair * 3 + row, 4, stride=ODD), :] = line[
                            :, at : at + LANES
                        ]
            return carry

        lax.fori_loop(0, pairs // 8, unpack, 0)

        def sink(n, carry, c=c):
            slot = slot_ref[n]
            target = jnp.minimum(slot, TOP_SLOTS - 1) * 2
            usable = jnp.where(slot < TOP_SLOTS, 1.0, 0.0).astype(F32)
            turn = pl.ds(octant_ref[n] * ODD, top_theta)
            for tile in range(3):
                cosine = cos_ref[tile, turn, :]
                sine = sin_ref[tile, turn, :]
                real = total_ref[tile, pl.ds(target * ODD, top_theta), :]
                imag = total_ref[tile, pl.ds((target + 1) * ODD, top_theta), :]
                turned = jnp.concatenate(
                    [
                        (cosine * real + sine * imag).astype(BF16),
                        (cosine * imag - sine * real).astype(BF16),
                    ],
                    axis=1,
                )
                narrowed = jnp.dot(theta_flip[...], turned, preferred_element_type=F32)
                narrowed = narrowed.astype(BF16)
                lanes = slice(tile * LANES, (tile + 1) * LANES)
                narrow_ref[:lower_theta, lanes] = narrowed[:, :LANES]
                narrow_ref[lower_theta:, lanes] = narrowed[:, LANES:]
            result = lax.dot_general(
                narrow_ref[...],
                azimuth_ref[...],
                (((1,), (1,)), ((), ())),
                preferred_element_type=F32,
            )
            out_ref[n, :, c] = (result * usable).astype(BF16).reshape(2, lower_theta, lower_phi)
            return carry

        lax.fori_loop(0, parent_count, sink, 0, unroll=2)

    for side, out in enumerate((up_send.at[0], up_send.at[1], down_send.at[0], down_send.at[1])):
        some = out.at[pl.ds(1, count - 1)]
        pltpu.make_async_copy(some, some, send_sem.at[side]).wait()


VMEM = pl.BlockSpec(memory_space=pltpu.VMEM)
SMEM = pl.BlockSpec(memory_space=pltpu.SMEM)
ANY = pl.BlockSpec(memory_space=pl.ANY)
LIMIT = 56 * 1024 * 1024


def shards(
    parents,
    theta_table,
    azimuth_table,
    phase_angle,
    translators,
    parent_slot,
    parent_octant,
    top_box,
    far_source,
    far_kind,
):
    top_theta, lower_theta = theta_table.shape
    devices = top_box.shape[0] // TOP_SLOTS
    boxes = far_source.shape[0]
    kinds = translators.shape[0]
    wire = pltpu.VMEM((COLUMNS, devices, 4, 640), BF16)
    rows = pltpu.VMEM((boxes * 18 + 8, LANES), F32)
    return pl.pallas_call(
        kernel,
        out_shape=jax.ShapeDtypeStruct(parents.shape, BF16),
        in_specs=[SMEM] * 2 + [VMEM] * 5 + [ANY] * 3,
        out_specs=VMEM,
        scratch_shapes=[
            pltpu.VMEM(phase_angle.shape, F32),
            pltpu.VMEM(parents.shape, BF16),
            pltpu.VMEM(translators.shape, F32),
            pltpu.VMEM((3, 8 * ODD + 8, LANES), F32),
            pltpu.VMEM((3, 8 * ODD + 8, LANES), F32),
            pltpu.VMEM((3, 4 * ODD + 4, LANES), F32),
            wire,
            wire,
            wire,
            wire,
            pltpu.VMEM((2,) + far_source.shape[::-1], jnp.int32),
            pltpu.SMEM(far_source.shape[::-1], jnp.int32),
            pltpu.SMEM(far_source.shape[::-1], jnp.int32),
            pltpu.VMEM((kinds * 18 + 8, LANES), F32),
            rows,
            rows,
            pltpu.VMEM((boxes * 2, 640), F32),
            pltpu.VMEM((boxes * 2, devices * 4), BF16),
            pltpu.VMEM((devices * 4, boxes * 2), BF16),
            pltpu.VMEM((lower_theta, top_theta), BF16),
            pltpu.VMEM((2 * lower_theta, azimuth_table.shape[1]), BF16),
            pltpu.SemaphoreType.DMA((5,)),
            pltpu.SemaphoreType.DMA((4,)),
            pltpu.SemaphoreType.DMA((4,)),
            pltpu.SemaphoreType.DMA((4,)),
        ],
        compiler_params=pltpu.CompilerParams(
            collective_id=0, has_side_effects=True, vmem_limit_bytes=LIMIT
        ),
    )(
        parent_slot,
        parent_octant,
        far_source.T,
        far_kind.T,
        top_box.reshape(1, -1),
        theta_table,
        azimuth_table,
        phase_angle,
        parents,
        translators,
    )


def solution(mesh):
    placed = (
        P(("grp", "dev"), None, None, None, None),
        P(),
        P(),
        P(),
        P(None, None, ("grp", "dev")),
        P(("grp", "dev")),
        P(("grp", "dev")),
        P(),
        P(),
        P(),
    )
    return jax.shard_map(
        shards,
        mesh=mesh,
        in_specs=placed,
        out_specs=P(("grp", "dev"), None, None, None, None),
        check_vma=False,
    )
```
